32 devices in a mesh: depth: 4 (over z), row: 8 (over y, x, core).
Axes of the slice: x: 2, y: 2, z: 4, core: 2. Of those that a mesh axis runs over, the one named last changes fastest.
Arguments:
- volume: float32 [128, 256, 4096], P('depth', 'row'), may hold values from 0.02 to 0.52
- palette: float32 [3, 8], replicated, may hold values from 0.15 to 4
Outputs:
- image: float32 [4, 256, 4096], P(None, 'row', 'depth')
The draws below stay inside these ranges and needn't reach their ends.
All inputs are finite; a program needn't handle non-finite values.
Results may differ from the reference program's by a relative error of at most 0.0003.
Values sent between devices are 32-bit elements; how exact they have to be, the bound alone decides.
A program may use at most 192 MiB of HBM per device.

```python
import jax
import jax.numpy as jnp
from jax import lax

CY = 32
NX = 4096
J = 8
NZ = 128
NY = 256


def draw_volume(key, part):
    choose_key = jax.random.fold_in(key, 11)
    level_key = jax.random.fold_in(key, 12)
    extent = (NZ, NY, NX)
    selector = jax.random.randint(choose_key, extent, 0, 4)
    levels = jax.random.uniform(level_key, extent, jnp.float32)
    sparse = 0.02 * jnp.exp(1.3862944 * levels)
    filled = 0.5 + 0.024 * (levels - 0.5)
    return jnp.where(selector == 0, sparse, filled).astype(jnp.float32)


def draw_palette(key, part):
    weak_key = jax.random.fold_in(key, 21)
    strong_key = jax.random.fold_in(key, 22)
    weaker = jax.random.uniform(weak_key, (3, J), jnp.float32, 0.2, 0.8)
    stronger = jax.random.uniform(strong_key, (3, J), jnp.float32, 2.5, 3.5)
    column = jnp.broadcast_to(jnp.arange(J)[None, :], (3, J))
    marked = (column == 1) | (column == J - 2)
    return jnp.where(marked, stronger, weaker).astype(jnp.float32)


def setup_inputs(seed: int = 0) -> dict:
    seeds = jax.random.split(jax.random.key(seed), 3)
    return {
        "volume": draw_volume(jax.random.fold_in(seeds[2], 71), 0),
        "palette": draw_palette(jax.random.fold_in(seeds[2], 71), 0),
    }


def sample_terms(field, grad_z, grad_y, grad_x, palette, scale):
    along = 0.36 * grad_z + 0.48 * grad_y + 0.8 * grad_x
    square = grad_z * grad_z + grad_y * grad_y + grad_x * grad_x
    shade = 0.25 + 0.75 * jnp.abs(along) / jnp.sqrt(square + 0.04)
    bumps = palette.shape[1]
    colors = [jnp.zeros_like(field) for k in range(3)]
    for j in range(bumps):
        bump = jnp.exp(-jnp.square((bumps - 1) * field - j))
        for k in range(3):
            colors[k] = colors[k] + palette[k, j] * bump
    colors = [shade * c for c in colors]
    return (field * scale, colors)

def reference(volume, palette):
    depth_cells, rows, columns = volume.shape
    scale = 4.0 / NZ

    def one_block(start):
        zero = jnp.int32(0)
        middle = lax.dynamic_slice(volume, (zero, start, zero), (depth_cells, CY, columns))
        above_row = jnp.maximum(start - 1, 0).astype(jnp.int32)
        below_row = jnp.minimum(start + CY, rows - 1).astype(jnp.int32)
        above = lax.dynamic_slice(volume, (zero, above_row, zero), (depth_cells, 1, columns))
        below = lax.dynamic_slice(volume, (zero, below_row, zero), (depth_cells, 1, columns))
        above = jnp.where(start > 0, above, jnp.zeros_like(above))
        below = jnp.where(start + CY < rows, below, jnp.zeros_like(below))
        extended = jnp.concatenate([above, middle, below], axis=1)
        padded = jnp.pad(middle, ((1, 1), (0, 0), (1, 1)))
        grad_z = (padded[2:, :, 1:-1] - padded[:-2, :, 1:-1]) * 0.5
        grad_y = (extended[:, 2:, :] - extended[:, :-2, :]) * 0.5
        grad_x = (padded[1:-1, :, 2:] - padded[1:-1, :, :-2]) * 0.5
        tau, colors = sample_terms(middle, grad_z, grad_y, grad_x, palette, scale)
        before = jnp.cumsum(tau, axis=0) - tau
        weight = jnp.exp(-before) * (1.0 - jnp.exp(-tau))
        channels = [lax.optimization_barrier(jnp.sum(weight * c, axis=0)) for c in colors]
        channels.append(1.0 - jnp.exp(-lax.optimization_barrier(jnp.sum(tau, axis=0))))
        return jnp.stack(channels, axis=0)
    starts = (jnp.arange(rows // CY) * CY).astype(jnp.int32)
    blocks = lax.map(one_block, starts)
    return jnp.transpose(blocks, (1, 0, 2, 3)).reshape(4, rows, columns)
```

```python
import functools
import math

import jax
import jax.numpy as jnp
from jax import lax
from jax.experimental import pallas as pl
from jax.experimental.pallas import tpu as pltpu
from jax.sharding import PartitionSpec as P

LANES = 128
TOP = 8
LOG2E = math.log2(math.e)
MESH = pl.DeviceIdType.MESH


def kernel(
    n, m, vol, pal, out, vb, part, from_left, from_right, y_send, y_recv,
    edge_sem, body_sem, z_send_sem, z_recv_sem, y_send_sem, y_recv_sem,
    r_send_sem, r_recv_sem, l_send_sem, l_recv_sem,
):
    depth, rows, columns = vol.shape
    chunks = columns // LANES
    per = chunks // n
    pieces = 2 if per % 2 == 0 else 1
    step = per // pieces
    tiles = rows // 8
    bumps = pal.shape[1]
    me = lax.axis_index("depth")
    row = lax.axis_index("row")
    has_front, has_back = me > 0, me < n - 1
    has_up, has_down = row > 0, row < m - 1
    front, back = {"depth": me - 1}, {"depth": me + 1}
    up, down = {"row": row - 1}, {"row": row + 1}
    sides = ((has_front, front), (has_back, back), (has_up, up), (has_down, down))

    is_last = jnp.where(me == n - 1, 1, 0)

    def block_at(k):
        return is_last * k + (1 - is_last) * (n - 1 - k)

    def edge_copy(end, c):
        z = 0 if end == 0 else depth - 1
        return pltpu.make_async_copy(
            vol.at[z, :, pl.ds(pl.multiple_of(c * LANES, LANES), LANES)],
            vb.at[z + 1, c + 1, pl.ds(TOP, rows), :],
            edge_sem.at[end, c],
        )

    def body_copy(c):
        return pltpu.make_async_copy(
            vol.at[pl.ds(1, depth - 2), :, pl.ds(pl.multiple_of(c * LANES, LANES), LANES)],
            vb.at[pl.ds(2, depth - 2), c + 1, pl.ds(TOP, rows), :],
            body_sem.at[c],
        )

    @pl.loop(0, chunks)
    def _(i):
        c = block_at(i // per) * per + i % per
        edge_copy(0, c).start()
        edge_copy(1, c).start()

    @pl.loop(0, chunks)
    def _(i):
        c = block_at(i // per) * per + i % per
        body_copy(c).start()

    barrier = pltpu.get_barrier_semaphore()
    for there, device in sides:
        @pl.when(there)
        def _():
            pl.semaphore_signal(barrier, inc=1, device_id=device, device_id_type=MESH)

    zeros = jnp.zeros((8, LANES), jnp.float32)

    @pl.loop(0, depth)
    def _(z):
        for t in range(tiles):
            vb[z + 1, 0, pl.ds(TOP + 8 * t, 8), :] = zeros
            vb[z + 1, chunks + 1, pl.ds(TOP + 8 * t, 8), :] = zeros

    for missing, plane in ((me == 0, 0), (me == n - 1, depth + 1)):
        @pl.when(missing)
        def _():
            @pl.loop(0, chunks)
            def _(c):
                for t in range(tiles):
                    vb[plane, c + 1, pl.ds(TOP + 8 * t, 8), :] = zeros

    for missing, at in ((row == 0, TOP - 1), (row == m - 1, TOP + rows)):
        @pl.when(missing)
        def _():
            @pl.loop(0, depth)
            def _(z):
                for b in range(n):
                    vb[z + 1, pl.ds(1 + b * per, per), at, :] = jnp.zeros((per, LANES), jnp.float32)

    count = sum(jnp.where(there, 1, 0) for there, _ in sides)
    pl.semaphore_wait(barrier, count)

    def z_copy(way, b):
        source, target, device = (1, depth + 1, front) if way == 0 else (depth, 0, back)
        cells = (pl.ds(1 + b * per, per), pl.ds(TOP, rows))
        return pltpu.make_async_remote_copy(
            src_ref=vb.at[source, cells[0], cells[1], :],
            dst_ref=vb.at[target, cells[0], cells[1], :],
            send_sem=z_send_sem.at[way, b],
            recv_sem=z_recv_sem.at[way, b],
            device_id=device,
            device_id_type=MESH,
        )

    def y_copy(way, b):
        return pltpu.make_async_remote_copy(
            src_ref=y_send.at[way, b],
            dst_ref=y_recv.at[way, b],
            send_sem=y_send_sem.at[way, b],
            recv_sem=y_recv_sem.at[way, b],
            device_id=up if way == 0 else down,
            device_id_type=MESH,
        )

    @pl.loop(0, n)
    def _(k):
        b = block_at(k)

        @pl.loop(0, per)
        def _(i):
            edge_copy(0, b * per + i).wait()
            edge_copy(1, b * per + i).wait()

        @pl.when(has_front)
        def _():
            z_copy(0, b).start()

        @pl.when(has_back)
        def _():
            z_copy(1, b).start()

    @pl.loop(0, n)
    def _(k):
        b = block_at(k)

        @pl.loop(0, per)
        def _(i):
            body_copy(b * per + i).wait()

        here = pl.ds(1 + b * per, per)
        for way, there, at in ((0, has_up, TOP), (1, has_down, TOP + rows - 1)):
            @pl.when(there)
            def _():
                @pl.loop(0, depth)
                def _(z):
                    y_send[way, b, z] = vb[z + 1, here, at, :]

                y_copy(way, b).start()

    lane = lax.broadcasted_iota(jnp.int32, (8, LANES), 1)
    first, last = lane == 0, lane == LANES - 1
    scale = 4.0 / (depth * n)
    wide = float(bumps - 1)
    along_gain = 0.6
    gains = [
        [pal[k, j] * (along_gain * math.exp(-float(j * j))) for j in range(bumps)]
        for k in range(3)
    ]

    def pixels(c, t):
        rows_here = pl.ds(pl.multiple_of(TOP + 8 * t, 8), 8)
        rows_up = pl.ds(TOP - 1 + 8 * t, 8)
        rows_down = pl.ds(TOP + 1 + 8 * t, 8)
        before = vb[0, c + 1, rows_here, :]
        here = vb[1, c + 1, rows_here, :]
        passed = None
        sums = [None] * bumps
        for z in range(1, depth + 1):
            after = vb[z + 1, c + 1, rows_here, :]
            dz = after - before
            dy = vb[z, c + 1, rows_down, :] - vb[z, c + 1, rows_up, :]
            left = jnp.where(last, vb[z, c, rows_here, :], here)
            right = jnp.where(first, vb[z, c + 2, rows_here, :], here)
            dx = pltpu.roll(right, LANES - 1, 1) - pltpu.roll(left, 1, 1)
            along = dx + 0.45 * dz + 0.6 * dy
            square = (dx * dx + 0.16) + (dy * dy + dz * dz)
            shade = jnp.abs(along) * lax.rsqrt(square) + 0.25 / along_gain
            clear = jnp.exp2(here * (-scale * LOG2E))
            power = jnp.exp2(here * (2.0 * wide * LOG2E))
            base = jnp.exp2((here * (-wide * wide * LOG2E)) * here)
            now = clear if passed is None else passed * clear
            weight = (1.0 if passed is None else passed) - now
            passed = now
            term = (weight * base) * shade
            for j in range(bumps):
                sums[j] = term if sums[j] is None else sums[j] + term
                if j < bumps - 1:
                    term = term * power
            before, here = here, after
        for k in range(3):
            total = gains[k][0] * sums[0]
            for j in range(1, bumps):
                total = total + gains[k][j] * sums[j]
            part[c, k, pl.ds(pl.multiple_of(8 * t, 8), 8), :] = total
        part[c, 3, pl.ds(pl.multiple_of(8 * t, 8), 8), :] = passed

    def right_copy(source, b, p):
        cells = pl.ds(b * per + p * step, step)
        return pltpu.make_async_remote_copy(
            src_ref=source.at[cells],
            dst_ref=from_left.at[cells],
            send_sem=r_send_sem.at[b, p],
            recv_sem=r_recv_sem.at[b, p],
            device_id=back,
            device_id_type=MESH,
        )

    def left_copy(source, b, p):
        cells = pl.ds(b * per + p * step, step)
        return pltpu.make_async_remote_copy(
            src_ref=source.at[cells],
            dst_ref=from_right.at[cells],
            send_sem=l_send_sem.at[b, p],
            recv_sem=l_recv_sem.at[b, p],
            device_id=front,
            device_id_type=MESH,
        )

    def take_halo(b):
        @pl.when(has_front)
        def _():
            z_copy(1, b).wait_recv()

        @pl.when(has_back)
        def _():
            z_copy(0, b).wait_recv()

        here = pl.ds(1 + b * per, per)
        for way, there, at in ((1, has_up, TOP - 1), (0, has_down, TOP + rows)):
            @pl.when(there)
            def _():
                y_copy(way, b).wait_recv()

                @pl.loop(0, depth)
                def _(z):
                    vb[z + 1, here, at, :] = y_recv[way, b, z]

    @pl.loop(0, n)
    def _(k):
        b = block_at(k)
        take_halo(b)

        @pl.loop(0, pieces)
        def _(p):
            @pl.loop(0, step * tiles)
            def _(i):
                pixels(b * per + p * step + i // tiles, i % tiles)

            @pl.when((me == 0) & (b > 0))
            def _():
                right_copy(part, b, p).start()

            @pl.when((me == n - 1) & (b < n - 1))
            def _():
                left_copy(part, b, p).start()

    def blend(c, t, ahead, behind, store):
        at = pl.ds(pl.multiple_of(8 * t, 8), 8)
        passes = ahead[c, 3, at, :]
        values = [ahead[c, k, at, :] + passes * behind[c, k, at, :] for k in range(3)]
        values.append(passes * behind[c, 3, at, :])
        for k in range(4):
            store[c, k, at, :] = values[k]

    def blend_piece(b, p, ahead, behind, store):
        @pl.loop(0, step * tiles)
        def _(i):
            blend(b * per + p * step + i // tiles, i % tiles, ahead, behind, store)

    for s in range(n - 1):
        for p in range(pieces):
            b = n - 1 - s

            @pl.when((me > 0) & (me < b))
            def _():
                right_copy(part, b, p).wait_recv()
                blend_piece(b, p, from_left, part, from_left)
                right_copy(from_left, b, p).start()

            a = s

            @pl.when((me > a) & (me < n - 1))
            def _():
                left_copy(part, a, p).wait_recv()
                blend_piece(a, p, part, from_right, from_right)
                left_copy(from_right, a, p).start()

    @pl.loop(0, pieces)
    def _(p):
        @pl.when(has_front)
        def _():
            right_copy(part, me, p).wait_recv()
            blend_piece(me, p, from_left, part, part)

        @pl.when(has_back)
        def _():
            left_copy(part, me, p).wait_recv()
            blend_piece(me, p, part, from_right, part)

    @pl.loop(0, tiles)
    def _(t):
        at = pl.ds(pl.multiple_of(8 * t, 8), 8)
        for i in range(per):
            for k in range(4):
                value = part[me * per + i, k, at, :]
                out[k, at, pl.ds(i * LANES, LANES)] = 1.0 - value if k == 3 else value

    @pl.loop(0, n)
    def _(b):
        @pl.when(has_front)
        def _():
            z_copy(0, b).wait_send()

        @pl.when(has_back)
        def _():
            z_copy(1, b).wait_send()

        @pl.when(has_up)
        def _():
            y_copy(0, b).wait_send()

        @pl.when(has_down)
        def _():
            y_copy(1, b).wait_send()

        @pl.loop(0, pieces)
        def _(p):
            @pl.when(me < b)
            def _():
                right_copy(part, b, p).wait_send()

            @pl.when(me > b)
            def _():
                left_copy(part, b, p).wait_send()


def on_device(volume, palette):
    depth, rows, columns = volume.shape
    n, m = lax.axis_size("depth"), lax.axis_size("row")
    chunks = columns // LANES
    per = chunks // n
    pieces = 2 if per % 2 == 0 else 1
    image = pltpu.VMEM((chunks, 4, rows, LANES), jnp.float32)
    sides = pltpu.VMEM((2, n, depth, per, LANES), jnp.float32)
    dma = pltpu.SemaphoreType.DMA
    return pl.pallas_call(
        functools.partial(kernel, n, m),
        out_shape=jax.ShapeDtypeStruct((4, rows, columns // n), jnp.float32),
        in_specs=[
            pl.BlockSpec(memory_space=pl.ANY),
            pl.BlockSpec(memory_space=pltpu.SMEM),
        ],
        out_specs=pl.BlockSpec(memory_space=pltpu.VMEM),
        scratch_shapes=[
            pltpu.VMEM((depth + 2, chunks + 2, rows + 16, LANES), jnp.float32),
            image, image, image, sides, sides,
            dma((2, chunks)), dma((chunks,)),
            dma((2, n)), dma((2, n)), dma((2, n)), dma((2, n)),
            dma((n, pieces)), dma((n, pieces)), dma((n, pieces)), dma((n, pieces)),
        ],
        compiler_params=pltpu.CompilerParams(
            collective_id=0, has_side_effects=True, vmem_limit_bytes=56 * 2**20
        ),
    )(volume, palette)


def solution(mesh):
    return jax.shard_map(
        on_device,
        mesh=mesh,
        in_specs=(P("depth", "row", None), P()),
        out_specs=P(None, "row", "depth"),
        check_vma=False,
    )
```

```python
import functools
import math

import jax
import jax.numpy as jnp
from jax import lax
from jax.experimental import pallas as pl
from jax.experimental.pallas import tpu as pltpu
from jax.sharding import PartitionSpec as P

LANES = 128
TOP = 8
LOG2E = math.log2(math.e)
MESH = pl.DeviceIdType.MESH


def kernel(
    n, m, vol, pal, out, vb, part, from_left, from_right, y_send, y_recv,
    edge_sem, body_sem, z_send_sem, z_recv_sem, y_send_sem, y_recv_sem,
    r_send_sem, r_recv_sem, l_send_sem, l_recv_sem,
):
    depth, rows, columns = vol.shape
    chunks = columns // LANES
    per = chunks // n
    pieces = 2 if per % 2 == 0 else 1
    step = per // pieces
    tiles = rows // 8
    bumps = pal.shape[1]
    me = lax.axis_index("depth")
    row = lax.axis_index("row")
    has_front, has_back = me > 0, me < n - 1
    has_up, has_down = row > 0, row < m - 1
    front, back = {"depth": me - 1}, {"depth": me + 1}
    up, down = {"row": row - 1}, {"row": row + 1}
    sides = ((has_front, front), (has_back, back), (has_up, up), (has_down, down))

    def block_of(device, k):
        rising = jnp.where(device >= n // 2, 1, 0)
        return rising * k + (1 - rising) * (n - 1 - k)

    def block_at(k):
        return block_of(me, k)

    def edge_copy(end, c):
        z = 0 if end == 0 else depth - 1
        return pltpu.make_async_copy(
            vol.at[z, :, pl.ds(pl.multiple_of(c * LANES, LANES), LANES)],
            vb.at[z + 1, c + 1, pl.ds(TOP, rows), :],
            edge_sem.at[end, c],
        )

    def body_copy(c):
        return pltpu.make_async_copy(
            vol.at[pl.ds(1, depth - 2), :, pl.ds(pl.multiple_of(c * LANES, LANES), LANES)],
            vb.at[pl.ds(2, depth - 2), c + 1, pl.ds(TOP, rows), :],
            body_sem.at[c],
        )

    @pl.loop(0, chunks)
    def _(i):
        c = block_at(i // per) * per + i % per
        edge_copy(0, c).start()
        edge_copy(1, c).start()

    @pl.loop(0, chunks)
    def _(i):
        c = block_at(i // per) * per + i % per
        body_copy(c).start()

    barrier = pltpu.get_barrier_semaphore()
    for there, device in sides:
        @pl.when(there)
        def _():
            pl.semaphore_signal(barrier, inc=1, device_id=device, device_id_type=MESH)

    zeros = jnp.zeros((8, LANES), jnp.float32)

    @pl.loop(0, depth)
    def _(z):
        for t in range(tiles):
            vb[z + 1, 0, pl.ds(TOP + 8 * t, 8), :] = zeros
            vb[z + 1, chunks + 1, pl.ds(TOP + 8 * t, 8), :] = zeros

    for missing, plane in ((me == 0, 0), (me == n - 1, depth + 1)):
        @pl.when(missing)
        def _():
            @pl.loop(0, chunks)
            def _(c):
                for t in range(tiles):
                    vb[plane, c + 1, pl.ds(TOP + 8 * t, 8), :] = zeros

    for missing, at in ((row == 0, TOP - 1), (row == m - 1, TOP + rows)):
        @pl.when(missing)
        def _():
            @pl.loop(0, depth)
            def _(z):
                for b in range(n):
                    vb[z + 1, pl.ds(1 + b * per, per), at, :] = jnp.zeros((per, LANES), jnp.float32)

    count = sum(jnp.where(there, 1, 0) for there, _ in sides)
    pl.semaphore_wait(barrier, count)

    def z_copy(way, b):
        source, target, device = (1, depth + 1, front) if way == 0 else (depth, 0, back)
        cells = (pl.ds(1 + b * per, per), pl.ds(TOP, rows))
        return pltpu.make_async_remote_copy(
            src_ref=vb.at[source, cells[0], cells[1], :],
            dst_ref=vb.at[target, cells[0], cells[1], :],
            send_sem=z_send_sem.at[way, b],
            recv_sem=z_recv_sem.at[way, b],
            device_id=device,
            device_id_type=MESH,
        )

    def y_copy(way, b):
        return pltpu.make_async_remote_copy(
            src_ref=y_send.at[way, b],
            dst_ref=y_recv.at[way, b],
            send_sem=y_send_sem.at[way, b],
            recv_sem=y_recv_sem.at[way, b],
            device_id=up if way == 0 else down,
            device_id_type=MESH,
        )

    @pl.loop(0, chunks)
    def _(c):
        edge_copy(0, c).wait()
        edge_copy(1, c).wait()

    @pl.loop(0, n)
    def _(k):
        b = block_at(k)

        @pl.when(has_front)
        def _():
            z_copy(0, block_of(me - 1, k)).start()

        @pl.when(has_back)
        def _():
            z_copy(1, block_of(me + 1, k)).start()

        @pl.loop(0, per)
        def _(i):
            body_copy(b * per + i).wait()

        here = pl.ds(1 + b * per, per)
        for way, there, at in ((0, has_up, TOP), (1, has_down, TOP + rows - 1)):
            @pl.when(there)
            def _():
                @pl.loop(0, depth)
                def _(z):
                    y_send[way, b, z] = vb[z + 1, here, at, :]

                y_copy(way, b).start()

    lane = lax.broadcasted_iota(jnp.int32, (8, LANES), 1)
    first, last = lane == 0, lane == LANES - 1
    scale = 4.0 / (depth * n)
    wide = float(bumps - 1)
    along_gain = 0.6
    gains = [
        [pal[k, j] * (along_gain * math.exp(-float(j * j))) for j in range(bumps)]
        for k in range(3)
    ]

    def pixels(c, t):
        rows_here = pl.ds(pl.multiple_of(TOP + 8 * t, 8), 8)
        rows_up = pl.ds(TOP - 1 + 8 * t, 8)
        rows_down = pl.ds(TOP + 1 + 8 * t, 8)
        before = vb[0, c + 1, rows_here, :]
        here = vb[1, c + 1, rows_here, :]
        passed = None
        sums = [None] * bumps
        for z in range(1, depth + 1):
            after = vb[z + 1, c + 1, rows_here, :]
            dz = after - before
            dy = vb[z, c + 1, rows_down, :] - vb[z, c + 1, rows_up, :]
            left = jnp.where(last, vb[z, c, rows_here, :], here)
            right = jnp.where(first, vb[z, c + 2, rows_here, :], here)
            dx = pltpu.roll(right, LANES - 1, 1) - pltpu.roll(left, 1, 1)
            along = dx + 0.45 * dz + 0.6 * dy
            square = (dx * dx + 0.16) + (dy * dy + dz * dz)
            shade = jnp.abs(along) * lax.rsqrt(square) + 0.25 / along_gain
            clear = jnp.exp2(here * (-scale * LOG2E))
            power = jnp.exp2(here * (2.0 * wide * LOG2E))
            base = jnp.exp2((here * (-wide * wide * LOG2E)) * here)
            now = clear if passed is None else passed * clear
            weight = (1.0 if passed is None else passed) - now
            passed = now
            term = (weight * base) * shade
            for j in range(bumps):
                sums[j] = term if sums[j] is None else sums[j] + term
                if j < bumps - 1:
                    term = term * power
            before, here = here, after
        for k in range(3):
            total = gains[k][0] * sums[0]
            for j in range(1, bumps):
                total = total + gains[k][j] * sums[j]
            part[c, k, pl.ds(pl.multiple_of(8 * t, 8), 8), :] = total
        part[c, 3, pl.ds(pl.multiple_of(8 * t, 8), 8), :] = passed

    def right_copy(source, b, p):
        cells = pl.ds(b * per + p * step, step)
        return pltpu.make_async_remote_copy(
            src_ref=source.at[cells],
            dst_ref=from_left.at[cells],
            send_sem=r_send_sem.at[b, p],
            recv_sem=r_recv_sem.at[b, p],
            device_id=back,
            device_id_type=MESH,
        )

    def left_copy(source, b, p):
        cells = pl.ds(b * per + p * step, step)
        return pltpu.make_async_remote_copy(
            src_ref=source.at[cells],
            dst_ref=from_right.at[cells],
            send_sem=l_send_sem.at[b, p],
            recv_sem=l_recv_sem.at[b, p],
            device_id=front,
            device_id_type=MESH,
        )

    def take_halo(b):
        @pl.when(has_front)
        def _():
            z_copy(1, b).wait_recv()

        @pl.when(has_back)
        def _():
            z_copy(0, b).wait_recv()

        here = pl.ds(1 + b * per, per)
        for way, there, at in ((1, has_up, TOP - 1), (0, has_down, TOP + rows)):
            @pl.when(there)
            def _():
                y_copy(way, b).wait_recv()

                @pl.loop(0, depth)
                def _(z):
                    vb[z + 1, here, at, :] = y_recv[way, b, z]

    def blend(c, t, ahead, behind, store):
        at = pl.ds(pl.multiple_of(8 * t, 8), 8)
        passes = ahead[c, 3, at, :]
        values = [ahead[c, k, at, :] + passes * behind[c, k, at, :] for k in range(3)]
        values.append(passes * behind[c, 3, at, :])
        for k in range(4):
            store[c, k, at, :] = values[k]

    def blend_piece(b, p, ahead, behind, store):
        @pl.loop(0, step * tiles)
        def _(i):
            blend(b * per + p * step + i // tiles, i % tiles, ahead, behind, store)

    def render(k):
        b = block_at(k)
        take_halo(b)

        @pl.loop(0, pieces)
        def _(p):
            @pl.loop(0, step * tiles)
            def _(i):
                pixels(b * per + p * step + i // tiles, i % tiles)

            @pl.when((me == 0) & (b > 0))
            def _():
                right_copy(part, b, p).start()

            @pl.when((me == n - 1) & (b < n - 1))
            def _():
                left_copy(part, b, p).start()

    def pass_on(turn):
        b = n - 1 - turn + me
        a = turn - (n - 1) + me

        @pl.loop(0, pieces)
        def _(p):
            @pl.when((me > 0) & (me < b) & (b < n))
            def _():
                right_copy(part, b, p).wait_recv()
                blend_piece(b, p, from_left, part, from_left)
                right_copy(from_left, b, p).start()

            @pl.when((me < n - 1) & (a >= 0) & (a < me))
            def _():
                left_copy(part, a, p).wait_recv()
                blend_piece(a, p, part, from_right, from_right)
                left_copy(from_right, a, p).start()

    @pl.loop(0, n)
    def _(k):
        render(k)

        @pl.when(k == max(n - 2, 0))
        def _():
            pass_on(1)

    @pl.loop(2, max(n - 1, 2))
    def _(turn):
        pass_on(turn)

    @pl.loop(0, pieces)
    def _(p):
        @pl.when(has_front)
        def _():
            right_copy(part, me, p).wait_recv()
            blend_piece(me, p, from_left, part, part)

        @pl.when(has_back)
        def _():
            left_copy(part, me, p).wait_recv()
            blend_piece(me, p, part, from_right, part)

    @pl.loop(0, tiles)
    def _(t):
        at = pl.ds(pl.multiple_of(8 * t, 8), 8)
        for i in range(per):
            for k in range(4):
                value = part[me * per + i, k, at, :]
                out[k, at, pl.ds(i * LANES, LANES)] = 1.0 - value if k == 3 else value

    @pl.loop(0, n)
    def _(b):
        @pl.when(has_front)
        def _():
            z_copy(0, b).wait_send()

        @pl.when(has_back)
        def _():
            z_copy(1, b).wait_send()

        @pl.when(has_up)
        def _():
            y_copy(0, b).wait_send()

        @pl.when(has_down)
        def _():
            y_copy(1, b).wait_send()

        @pl.loop(0, pieces)
        def _(p):
            @pl.when(me < b)
            def _():
                right_copy(part, b, p).wait_send()

            @pl.when(me > b)
            def _():
                left_copy(part, b, p).wait_send()


def on_device(volume, palette):
    depth, rows, columns = volume.shape
    n, m = lax.axis_size("depth"), lax.axis_size("row")
    chunks = columns // LANES
    per = chunks // n
    pieces = 2 if per % 2 == 0 else 1
    image = pltpu.VMEM((chunks, 4, rows, LANES), jnp.float32)
    sides = pltpu.VMEM((2, n, depth, per, LANES), jnp.float32)
    dma = pltpu.SemaphoreType.DMA
    return pl.pallas_call(
        functools.partial(kernel, n, m),
        out_shape=jax.ShapeDtypeStruct((4, rows, columns // n), jnp.float32),
        in_specs=[
            pl.BlockSpec(memory_space=pl.ANY),
            pl.BlockSpec(memory_space=pltpu.SMEM),
        ],
        out_specs=pl.BlockSpec(memory_space=pltpu.VMEM),
        scratch_shapes=[
            pltpu.VMEM((depth + 2, chunks + 2, rows + 16, LANES), jnp.float32),
            image, image, image, sides, sides,
            dma((2, chunks)), dma((chunks,)),
            dma((2, n)), dma((2, n)), dma((2, n)), dma((2, n)),
            dma((n, pieces)), dma((n, pieces)), dma((n, pieces)), dma((n, pieces)),
        ],
        compiler_params=pltpu.CompilerParams(
            collective_id=0, has_side_effects=True, vmem_limit_bytes=56 * 2**20
        ),
    )(volume, palette)


def solution(mesh):
    return jax.shard_map(
        on_device,
        mesh=mesh,
        in_specs=(P("depth", "row", None), P()),
        out_specs=P(None, "row", "depth"),
        check_vma=False,
    )
```

```python
import functools
import math

import jax
import jax.numpy as jnp
from jax import lax
from jax.experimental import pallas as pl
from jax.experimental.pallas import tpu as pltpu
from jax.sharding import PartitionSpec as P

LANES = 128
TOP = 8
LOG2E = math.log2(math.e)
MESH = pl.DeviceIdType.MESH


def kernel(
    n, m, vol, pal, out, vb, part, from_left, from_right, y_send, y_recv,
    edge_sem, body_sem, z_send_sem, z_recv_sem, y_send_sem, y_recv_sem,
    r_send_sem, r_recv_sem, l_send_sem, l_recv_sem,
):
    depth, rows, columns = vol.shape
    chunks = columns // LANES
    per = chunks // n
    pieces = 4 if per % 4 == 0 else 1
    step = per // pieces
    tiles = rows // 8
    bumps = pal.shape[1]
    me = lax.axis_index("depth")
    row = lax.axis_index("row")
    has_front, has_back = me > 0, me < n - 1
    has_up, has_down = row > 0, row < m - 1
    front, back = {"depth": me - 1}, {"depth": me + 1}
    up, down = {"row": row - 1}, {"row": row + 1}
    sides = ((has_front, front), (has_back, back), (has_up, up), (has_down, down))

    def block_of(device, k):
        rising = jnp.where(device >= n // 2, 1, 0)
        return rising * k + (1 - rising) * (n - 1 - k)

    def block_at(k):
        return block_of(me, k)

    def edge_copy(end, c):
        z = 0 if end == 0 else depth - 1
        return pltpu.make_async_copy(
            vol.at[z, :, pl.ds(pl.multiple_of(c * LANES, LANES), LANES)],
            vb.at[z + 1, c + 1, pl.ds(TOP, rows), :],
            edge_sem.at[end, c],
        )

    def body_copy(c):
        return pltpu.make_async_copy(
            vol.at[pl.ds(1, depth - 2), :, pl.ds(pl.multiple_of(c * LANES, LANES), LANES)],
            vb.at[pl.ds(2, depth - 2), c + 1, pl.ds(TOP, rows), :],
            body_sem.at[c],
        )

    @pl.loop(0, chunks)
    def _(i):
        c = block_at(i // per) * per + i % per
        edge_copy(0, c).start()
        edge_copy(1, c).start()

    @pl.loop(0, chunks)
    def _(i):
        c = block_at(i // per) * per + i % per
        body_copy(c).start()

    barrier = pltpu.get_barrier_semaphore()
    for there, device in sides:
        @pl.when(there)
        def _():
            pl.semaphore_signal(barrier, inc=1, device_id=device, device_id_type=MESH)

    zeros = jnp.zeros((8, LANES), jnp.float32)

    @pl.loop(0, depth)
    def _(z):
        for t in range(tiles):
            vb[z + 1, 0, pl.ds(TOP + 8 * t, 8), :] = zeros
            vb[z + 1, chunks + 1, pl.ds(TOP + 8 * t, 8), :] = zeros

    for missing, plane in ((me == 0, 0), (me == n - 1, depth + 1)):
        @pl.when(missing)
        def _():
            @pl.loop(0, chunks)
            def _(c):
                for t in range(tiles):
                    vb[plane, c + 1, pl.ds(TOP + 8 * t, 8), :] = zeros

    for missing, at in ((row == 0, TOP - 1), (row == m - 1, TOP + rows)):
        @pl.when(missing)
        def _():
            @pl.loop(0, depth)
            def _(z):
                for b in range(n):
                    vb[z + 1, pl.ds(1 + b * per, per), at, :] = jnp.zeros((per, LANES), jnp.float32)

    count = sum(jnp.where(there, 1, 0) for there, _ in sides)
    pl.semaphore_wait(barrier, count)

    def z_copy(way, b):
        source, target, device = (1, depth + 1, front) if way == 0 else (depth, 0, back)
        cells = (pl.ds(1 + b * per, per), pl.ds(TOP, rows))
        return pltpu.make_async_remote_copy(
            src_ref=vb.at[source, cells[0], cells[1], :],
            dst_ref=vb.at[target, cells[0], cells[1], :],
            send_sem=z_send_sem.at[way, b],
            recv_sem=z_recv_sem.at[way, b],
            device_id=device,
            device_id_type=MESH,
        )

    def y_copy(way, b):
        return pltpu.make_async_remote_copy(
            src_ref=y_send.at[way, b],
            dst_ref=y_recv.at[way, b],
            send_sem=y_send_sem.at[way, b],
            recv_sem=y_recv_sem.at[way, b],
            device_id=up if way == 0 else down,
            device_id_type=MESH,
        )

    @pl.loop(0, chunks)
    def _(c):
        edge_copy(0, c).wait()
        edge_copy(1, c).wait()

    def send_planes(k):
        @pl.when(has_front)
        def _():
            z_copy(0, block_of(me - 1, k)).start()

        @pl.when(has_back)
        def _():
            z_copy(1, block_of(me + 1, k)).start()

    def send_rows(k):
        b = block_at(k)

        @pl.loop(0, per)
        def _(i):
            body_copy(b * per + i).wait()

        here = pl.ds(1 + b * per, per)
        for way, there, at in ((0, has_up, TOP), (1, has_down, TOP + rows - 1)):
            @pl.when(there)
            def _():
                @pl.loop(0, depth)
                def _(z):
                    y_send[way, b, z] = vb[z + 1, here, at, :]

                y_copy(way, b).start()

    ahead_blocks = min(2, n)

    @pl.loop(0, ahead_blocks)
    def _(k):
        send_planes(k)
        send_rows(k)

    @pl.loop(ahead_blocks, n)
    def _(k):
        send_planes(k)

    lane = lax.broadcasted_iota(jnp.int32, (8, LANES), 1)
    first, last = lane == 0, lane == LANES - 1
    scale = 4.0 / (depth * n)
    wide = float(bumps - 1)
    along_gain = 0.6
    gains = [
        [pal[k, j] * (along_gain * math.exp(-float(j * j))) for j in range(bumps)]
        for k in range(3)
    ]

    def pixels(c, t):
        rows_here = pl.ds(pl.multiple_of(TOP + 8 * t, 8), 8)
        rows_up = pl.ds(TOP - 1 + 8 * t, 8)
        rows_down = pl.ds(TOP + 1 + 8 * t, 8)
        before = vb[0, c + 1, rows_here, :]
        here = vb[1, c + 1, rows_here, :]
        passed = None
        sums = [None] * bumps
        for z in range(1, depth + 1):
            after = vb[z + 1, c + 1, rows_here, :]
            dz = after - before
            dy = vb[z, c + 1, rows_down, :] - vb[z, c + 1, rows_up, :]
            left = jnp.where(last, vb[z, c, rows_here, :], here)
            right = jnp.where(first, vb[z, c + 2, rows_here, :], here)
            dx = pltpu.roll(right, LANES - 1, 1) - pltpu.roll(left, 1, 1)
            along = dx + 0.45 * dz + 0.6 * dy
            square = (dx * dx + 0.16) + (dy * dy + dz * dz)
            shade = jnp.abs(along) * lax.rsqrt(square) + 0.25 / along_gain
            clear = jnp.exp2(here * (-scale * LOG2E))
            power = jnp.exp2(here * (2.0 * wide * LOG2E))
            base = jnp.exp2((here * (-wide * wide * LOG2E)) * here)
            now = clear if passed is None else passed * clear
            weight = (1.0 if passed is None else passed) - now
            passed = now
            term = (weight * base) * shade
            for j in range(bumps):
                sums[j] = term if sums[j] is None else sums[j] + term
                if j < bumps - 1:
                    term = term * power
            before, here = here, after
        for k in range(3):
            total = gains[k][0] * sums[0]
            for j in range(1, bumps):
                total = total + gains[k][j] * sums[j]
            part[c, k, pl.ds(pl.multiple_of(8 * t, 8), 8), :] = total
        part[c, 3, pl.ds(pl.multiple_of(8 * t, 8), 8), :] = passed

    def right_copy(source, b, p):
        cells = pl.ds(b * per + p * step, step)
        return pltpu.make_async_remote_copy(
            src_ref=source.at[cells],
            dst_ref=from_left.at[cells],
            send_sem=r_send_sem.at[b, p],
            recv_sem=r_recv_sem.at[b, p],
            device_id=back,
            device_id_type=MESH,
        )

    def left_copy(source, b, p):
        cells = pl.ds(b * per + p * step, step)
        return pltpu.make_async_remote_copy(
            src_ref=source.at[cells],
            dst_ref=from_right.at[cells],
            send_sem=l_send_sem.at[b, p],
            recv_sem=l_recv_sem.at[b, p],
            device_id=front,
            device_id_type=MESH,
        )

    def take_halo(b):
        @pl.when(has_front)
        def _():
            z_copy(1, b).wait_recv()

        @pl.when(has_back)
        def _():
            z_copy(0, b).wait_recv()

        here = pl.ds(1 + b * per, per)
        for way, there, at in ((1, has_up, TOP - 1), (0, has_down, TOP + rows)):
            @pl.when(there)
            def _():
                y_copy(way, b).wait_recv()

                @pl.loop(0, depth)
                def _(z):
                    vb[z + 1, here, at, :] = y_recv[way, b, z]

    def blend(c, t, ahead, behind, store):
        at = pl.ds(pl.multiple_of(8 * t, 8), 8)
        passes = ahead[c, 3, at, :]
        values = [ahead[c, k, at, :] + passes * behind[c, k, at, :] for k in range(3)]
        values.append(passes * behind[c, 3, at, :])
        for k in range(4):
            store[c, k, at, :] = values[k]

    def blend_piece(b, p, ahead, behind, store):
        @pl.loop(0, step * tiles)
        def _(i):
            blend(b * per + p * step + i // tiles, i % tiles, ahead, behind, store)

    def render(k):
        b = block_at(k)
        take_halo(b)

        @pl.loop(0, pieces)
        def _(p):
            @pl.loop(0, step * tiles)
            def _(i):
                pixels(b * per + p * step + i // tiles, i % tiles)

            @pl.when((me == 0) & (b > 0))
            def _():
                right_copy(part, b, p).start()

            @pl.when((me == n - 1) & (b < n - 1))
            def _():
                left_copy(part, b, p).start()

    def pass_on(turn):
        b = n - 1 - turn + me
        a = turn - (n - 1) + me

        @pl.loop(0, pieces)
        def _(p):
            @pl.when((me > 0) & (me < b) & (b < n))
            def _():
                right_copy(part, b, p).wait_recv()
                blend_piece(b, p, from_left, part, from_left)
                right_copy(from_left, b, p).start()

            @pl.when((me < n - 1) & (a >= 0) & (a < me))
            def _():
                left_copy(part, a, p).wait_recv()
                blend_piece(a, p, part, from_right, from_right)
                left_copy(from_right, a, p).start()

    @pl.loop(0, n)
    def _(k):
        render(k)

        @pl.when(k + ahead_blocks < n)
        def _():
            send_rows(k + ahead_blocks)

        @pl.when(k == max(n - 2, 0))
        def _():
            pass_on(1)

    @pl.loop(2, max(n - 1, 2))
    def _(turn):
        pass_on(turn)

    @pl.loop(0, pieces)
    def _(p):
        @pl.when(has_front)
        def _():
            right_copy(part, me, p).wait_recv()
            blend_piece(me, p, from_left, part, part)

        @pl.when(has_back)
        def _():
            left_copy(part, me, p).wait_recv()
            blend_piece(me, p, part, from_right, part)

    @pl.loop(0, tiles)
    def _(t):
        at = pl.ds(pl.multiple_of(8 * t, 8), 8)
        for i in range(per):
            for k in range(4):
                value = part[me * per + i, k, at, :]
                out[k, at, pl.ds(i * LANES, LANES)] = 1.0 - value if k == 3 else value

    @pl.loop(0, n)
    def _(b):
        @pl.when(has_front)
        def _():
            z_copy(0, b).wait_send()

        @pl.when(has_back)
        def _():
            z_copy(1, b).wait_send()

        @pl.when(has_up)
        def _():
            y_copy(0, b).wait_send()

        @pl.when(has_down)
        def _():
            y_copy(1, b).wait_send()

        @pl.loop(0, pieces)
        def _(p):
            @pl.when(me < b)
            def _():
                right_copy(part, b, p).wait_send()

            @pl.when(me > b)
            def _():
                left_copy(part, b, p).wait_send()


def on_device(volume, palette):
    depth, rows, columns = volume.shape
    n, m = lax.axis_size("depth"), lax.axis_size("row")
    chunks = columns // LANES
    per = chunks // n
    pieces = 4 if per % 4 == 0 else 1
    image = pltpu.VMEM((chunks, 4, rows, LANES), jnp.float32)
    sides = pltpu.VMEM((2, n, depth, per, LANES), jnp.float32)
    dma = pltpu.SemaphoreType.DMA
    return pl.pallas_call(
        functools.partial(kernel, n, m),
        out_shape=jax.ShapeDtypeStruct((4, rows, columns // n), jnp.float32),
        in_specs=[
            pl.BlockSpec(memory_space=pl.ANY),
            pl.BlockSpec(memory_space=pltpu.SMEM),
        ],
        out_specs=pl.BlockSpec(memory_space=pltpu.VMEM),
        scratch_shapes=[
            pltpu.VMEM((depth + 2, chunks + 2, rows + 16, LANES), jnp.float32),
            image, image, image, sides, sides,
            dma((2, chunks)), dma((chunks,)),
            dma((2, n)), dma((2, n)), dma((2, n)), dma((2, n)),
            dma((n, pieces)), dma((n, pieces)), dma((n, pieces)), dma((n, pieces)),
        ],
        compiler_params=pltpu.CompilerParams(
            collective_id=0, has_side_effects=True, vmem_limit_bytes=56 * 2**20
        ),
    )(volume, palette)


def solution(mesh):
    return jax.shard_map(
        on_device,
        mesh=mesh,
        in_specs=(P("depth", "row", None), P()),
        out_specs=P(None, "row", "depth"),
        check_vma=False,
    )
```
